1024 devices in a mesh: dp: 32 (over z), expert: 32 (over y, x, core).
Axes of the slice: x: 4, y: 4, z: 32, core: 2. Of those that a mesh axis runs over, the one named last changes fastest.
Arguments:
- tokens: bfloat16 [10240, 1664], P('dp', 'expert'), may hold values from -6 to 6
- cotangent: bfloat16 [10240, 1664], P('dp', 'expert'), may hold values from -6 to 6
- gate_values: bfloat16 [10240, 2], P('dp'), may hold values from 0.049804688 to 1
- route_ids: int32 [10240, 2], P('dp'), may hold values from 0 to 31, as said below
- route_slots: int32 [10240, 2], P('dp'), may hold values from 0 to 20, as said below
- kept_mask: int32 [10240, 2], P('dp'), may hold values from 0 to 1, as said below
- weight_in: bfloat16 [32, 1664, 8192], P('expert', None, 'dp'), may hold values from -0.15625 to 0.15625
- weight_out: bfloat16 [32, 8192, 1664], P('expert', 'dp'), may hold values from -0.0625 to 0.0625
Outputs:
- grad_tokens: bfloat16 [10240, 1664], P('dp', 'expert')
- grad_gates: float32 [10240, 2], P('dp')
- grad_in: bfloat16 [32, 1664, 8192], P('expert', None, 'dp')
- grad_out: bfloat16 [32, 8192, 1664], P('expert', 'dp')
The draws below stay inside these ranges and needn't reach their ends.
Inputs may be any that keep to these rules, and one draw needn't show every extreme that they name: `route_ids`: the two experts of a token differ; which experts are busy differs from group to group of 320 tokens. `route_slots`: within one group of 320 tokens, the kept assignments to one expert hold distinct slots; first choices take slots in priority order, then second choices fill the slots left; a dropped assignment has slot 0. `kept_mask`: an assignment is 0 exactly when its expert's 21 slots of its group were already taken.
All inputs are finite; a program needn't handle non-finite values.
Results may differ from the reference program's by a relative error of at most 0.0057.
Values may be sent and summed in bfloat16 or wider, within the bound.
No kernel may reach another device: no remote copies, remote signals or barrier semaphores. Data moves between devices by JAX's collectives and lax.ppermute only.
A program may use at most 32 MiB of HBM per device.

```python
import math
import jax
import jax.numpy as jnp
from jax import lax

D = 1664
FF = 8192
TOP = 2
TOK_ROW = 320
EXPERTS = 32
TOKENS = 10240
CAP = 21
N_DP = 32


def routing_draw(key):
    key_list = jax.random.split(key, 4)
    picks = jax.random.randint(key_list[0], (N_DP, TOK_ROW, 3), 0, EXPERTS)
    ranked = jnp.min(picks, axis=-1)
    relabel = jax.vmap(lambda sub_key: jax.random.permutation(sub_key, EXPERTS))(jax.random.split(key_list[1], N_DP))
    first_pick = jnp.take_along_axis(relabel, ranked, axis=1).astype(jnp.int32)
    offsets = jax.random.randint(key_list[2], (N_DP, TOK_ROW), 1, EXPERTS)
    second_pick = ((first_pick + offsets) % EXPERTS).astype(jnp.int32)
    priority = jax.vmap(lambda sub_key: jax.random.permutation(sub_key, TOK_ROW))(jax.random.split(key_list[3], N_DP))
    inverse = jnp.argsort(priority, axis=1)
    columns = jnp.arange(EXPERTS, dtype=jnp.int32)
    first_sorted = jnp.take_along_axis(first_pick, priority, axis=1)
    first_onehot = (first_sorted[:, :, None] == columns[None, None, :]).astype(jnp.int32)
    first_rank = jnp.sum(jnp.cumsum(first_onehot, axis=1) * first_onehot, axis=2) - 1
    first_fill = jnp.minimum(jnp.sum(first_onehot, axis=1), CAP)
    second_sorted = jnp.take_along_axis(second_pick, priority, axis=1)
    second_onehot = (second_sorted[:, :, None] == columns[None, None, :]).astype(jnp.int32)
    second_rank = jnp.sum(jnp.cumsum(second_onehot, axis=1) * second_onehot, axis=2) - 1
    second_slot = jnp.take_along_axis(first_fill, second_sorted, axis=1) + second_rank
    first_keep = first_rank < CAP
    second_keep = second_slot < CAP
    slots_sorted = jnp.stack([jnp.where(first_keep, first_rank, 0), jnp.where(second_keep, second_slot, 0)], axis=-1)
    keep_sorted = jnp.stack([first_keep, second_keep], axis=-1).astype(jnp.int32)
    slots = jnp.take_along_axis(slots_sorted, inverse[:, :, None], axis=1)
    keeps = jnp.take_along_axis(keep_sorted, inverse[:, :, None], axis=1)
    choices_made = jnp.stack([first_pick, second_pick], axis=-1)
    return (choices_made.reshape(TOKENS, TOP).astype(jnp.int32), slots.reshape(TOKENS, TOP).astype(jnp.int32), keeps.reshape(TOKENS, TOP).astype(jnp.int32))


def draw_route_ids(key, part):
    return routing_draw(key)[0]


def draw_route_slots(key, part):
    return routing_draw(key)[1]


def draw_kept_mask(key, part):
    return routing_draw(key)[2]


def steps_of(own_key, dims, pieces, smallest, top_value):
    level, own = 1.0, jax.random.fold_in(own_key, 6)
    for axis_at, parts in pieces:
        draws = jnp.exp(jax.random.uniform(jax.random.fold_in(own, axis_at), (parts,), jnp.float32, smallest / len(pieces), top_value / len(pieces)))
        level = level * jnp.repeat(draws, dims[axis_at] // parts).reshape([-1 if axis == axis_at else 1 for axis in range(len(dims))])
    return level


def scatter_about(key, dims, spread, bound, cuts=(), kind=jnp.bfloat16):
    gain = steps_of(key, dims, cuts, -0.22, 0.18) if cuts else 1.0
    drawn = jax.random.normal(key, dims, jnp.float32) * spread * gain
    return jnp.minimum(jnp.maximum(drawn, -bound), bound).astype(kind)


def setup_inputs(seed: int = 0) -> dict:
    keys = jax.random.split(jax.random.key(seed), 9)
    tokens = scatter_about(keys[0], (TOKENS, D), 1.0, 6.0, ((0, 32), (1, 32)))
    cotangent = scatter_about(keys[1], (TOKENS, D), 1.0, 6.0, ((0, 32), (1, 32)))
    gate_values = jnp.clip(jnp.exp(math.log(1.0) - 2.9996462 * jax.random.uniform(keys[2], (TOKENS, TOP), jnp.float32) ** steps_of(keys[2], (TOKENS, TOP), ((0, 32),), -0.2, 0.2)), 0.049804688, 1.0).astype(jnp.bfloat16)
    route_ids = draw_route_ids(jax.random.fold_in(keys[8], 71), 0)
    route_slots = draw_route_slots(jax.random.fold_in(keys[8], 71), 0)
    kept_mask = draw_kept_mask(jax.random.fold_in(keys[8], 71), 0)
    weight_in = scatter_about(keys[6], (EXPERTS, D, FF), D ** -0.5, 0.15625, ((0, 32), (2, 32)))
    weight_out = scatter_about(keys[7], (EXPERTS, FF, D), FF ** -0.5, 0.0625, ((0, 32), (1, 32)))
    return {"tokens": tokens, "cotangent": cotangent, "gate_values": gate_values, "route_ids": route_ids, "route_slots": route_slots, "kept_mask": kept_mask, "weight_in": weight_in, "weight_out": weight_out}


def gelu_exact(values):
    return 0.5 * values * (1.0 + jax.scipy.special.erf(values / math.sqrt(2.0)))

def gelu_slope(values):
    cumul = 0.5 * (1.0 + jax.scipy.special.erf(values / math.sqrt(2.0)))
    density = jnp.exp(-0.5 * values * values) / math.sqrt(2.0 * math.pi)
    return cumul + values * density

def routing_map(route_ids, route_slots, kept_mask, capacity, slot_total):
    target = route_ids * capacity + route_slots
    columns = jnp.arange(slot_total, dtype=jnp.int32)
    matches = (target[:, :, None] == columns[None, None, :]) & (kept_mask[:, :, None] == 1)
    return matches.astype(jnp.float32)

def reference(tokens, cotangent, gate_values, route_ids, route_slots, kept_mask, weight_in, weight_out):
    slot_total = EXPERTS * CAP
    f_local = FF // N_DP
    token_blocks = tokens.reshape(N_DP, TOK_ROW, D)
    grad_blocks = cotangent.reshape(N_DP, TOK_ROW, D)
    gate_blocks = gate_values.reshape(N_DP, TOK_ROW, TOP)
    id_blocks = route_ids.reshape(N_DP, TOK_ROW, TOP)
    slot_blocks = route_slots.reshape(N_DP, TOK_ROW, TOP)
    mask_blocks = kept_mask.reshape(N_DP, TOK_ROW, TOP)

    def dispatch(block):
        row_block, grad_block, gate_block, id_block, slot_block, mask_block = block
        matches = routing_map(id_block, slot_block, mask_block, CAP, slot_total)
        combine_map = lax.optimization_barrier(jnp.sum(matches, axis=1)).astype(jnp.bfloat16)
        row_buffer = jnp.dot(combine_map.T, row_block, preferred_element_type=jnp.float32).astype(jnp.bfloat16)
        grad_buffer = jnp.dot(combine_map.T, grad_block, preferred_element_type=jnp.float32).astype(jnp.bfloat16)
        gate_buffer = jnp.einsum('tks,tk->s', matches, gate_block.astype(jnp.float32)).astype(jnp.bfloat16)
        return (row_buffer, grad_buffer, gate_buffer)
    row_buffers, grad_buffers, gate_buffers = lax.map(dispatch, (token_blocks, grad_blocks, gate_blocks, id_blocks, slot_blocks, mask_blocks))
    row_experts = row_buffers.reshape(N_DP, EXPERTS, CAP, D).transpose(1, 0, 2, 3).reshape(EXPERTS, N_DP * CAP, D)
    grad_experts = grad_buffers.reshape(N_DP, EXPERTS, CAP, D).transpose(1, 0, 2, 3).reshape(EXPERTS, N_DP * CAP, D)
    gate_experts = gate_buffers.reshape(N_DP, EXPERTS, CAP).transpose(1, 0, 2).reshape(EXPERTS, N_DP * CAP)

    def expert_pass(block):
        expert_rows, expert_grads, expert_gates, first_weight, second_weight = block
        row_count = expert_rows.shape[0]
        pre_act = jnp.dot(expert_rows, first_weight, preferred_element_type=jnp.float32)
        hidden = gelu_exact(pre_act)
        grad_raw = jnp.dot(expert_grads, second_weight.T, preferred_element_type=jnp.float32)
        gate_terms = lax.optimization_barrier(jnp.sum((hidden * grad_raw).reshape(row_count, N_DP, f_local), axis=2))
        gate_grad = lax.optimization_barrier(jnp.sum(gate_terms, axis=1)).astype(jnp.bfloat16)
        scale = expert_gates.astype(jnp.float32)[:, None]
        grad_pre = (scale * grad_raw * gelu_slope(pre_act)).astype(jnp.bfloat16)
        hidden_low = hidden.astype(jnp.bfloat16)
        scaled_grads = (scale * expert_grads.astype(jnp.float32)).astype(jnp.bfloat16)
        grad_second = jnp.dot(hidden_low.T, scaled_grads, preferred_element_type=jnp.float32).astype(jnp.bfloat16)
        grad_first = jnp.dot(expert_rows.T, grad_pre, preferred_element_type=jnp.float32).astype(jnp.bfloat16)
        row_terms = jnp.einsum('rkf,dkf->rkd', grad_pre.reshape(row_count, N_DP, f_local).astype(jnp.float32), first_weight.reshape(D, N_DP, f_local).astype(jnp.float32))
        grad_rows = lax.optimization_barrier(jnp.sum(row_terms, axis=1)).astype(jnp.bfloat16)
        return (grad_rows, gate_grad, grad_first, grad_second)
    grad_rows, gate_grad, grad_in, grad_out = lax.map(expert_pass, (row_experts, grad_experts, gate_experts, weight_in, weight_out))
    rows_back = grad_rows.reshape(EXPERTS, N_DP, CAP, D).transpose(1, 0, 2, 3).reshape(N_DP, slot_total, D)
    gates_back = gate_grad.reshape(EXPERTS, N_DP, CAP).transpose(1, 0, 2).reshape(N_DP, slot_total)

    def combine(block):
        id_block, slot_block, mask_block, row_back, gate_back = block
        matches = routing_map(id_block, slot_block, mask_block, CAP, slot_total)
        combine_map = lax.optimization_barrier(jnp.sum(matches, axis=1)).astype(jnp.bfloat16)
        token_grads = jnp.dot(combine_map, row_back, preferred_element_type=jnp.float32).astype(jnp.bfloat16)
        gate_out = jnp.einsum('tks,s->tk', matches, gate_back.astype(jnp.float32))
        return (token_grads, gate_out)
    token_grads, gate_out = lax.map(combine, (id_blocks, slot_blocks, mask_blocks, rows_back, gates_back))
    return (token_grads.reshape(TOKENS, D), gate_out.reshape(TOKENS, TOP).astype(jnp.float32), grad_in, grad_out)
```

```python
import math

import jax
import jax.numpy as jnp
from jax import lax
from jax.sharding import PartitionSpec as P

BF16 = jnp.bfloat16
F32 = jnp.float32


def gelu_pair(values):
    cumul = 0.5 * (1.0 + lax.erf(values * (1.0 / math.sqrt(2.0))))
    density = jnp.exp(-0.5 * values * values) * (1.0 / math.sqrt(2.0 * math.pi))
    return values * cumul, cumul + values * density


def dot(left, right, dims):
    return lax.dot_general(left, right, ((dims[0], dims[1]), ((), ())), preferred_element_type=F32)


def body(tokens, cotangent, gate_values, route_ids, route_slots, kept_mask, weight_in, weight_out):
    experts = lax.axis_size("expert")
    dp = lax.axis_size("dp")
    half = dp // 2
    tok_rows, piece = tokens.shape
    width = piece * experts
    top = route_ids.shape[1]
    cap = (21 * top * tok_rows + 20 * experts - 1) // (20 * experts)
    pad = (cap + 1 + 7) // 8 * 8
    ring_cut = max(128, width * 5 // 8 // 128 * 128)
    me = lax.axis_index("expert")
    spot = lax.axis_index("dp") // 2
    mates = [(i, i ^ 1) for i in range(dp)]
    back = [(i, (i - 2) % dp) for i in range(dp)]
    groups = [list(range(0, dp, 2)), list(range(1, dp, 2))]

    own_in, own_out = weight_in[0], weight_out[0]
    mate_in = lax.ppermute(own_in, "dp", mates)
    mate_out = lax.ppermute(own_out, "dp", mates)

    kept = kept_mask == 1
    target = jnp.where(kept, route_ids * pad + route_slots, -1)
    slots = jnp.arange(experts * pad, dtype=jnp.int32)
    both = jnp.concatenate([tokens, cotangent], axis=1)
    spread = jnp.zeros((experts * pad, tok_rows), jnp.bool_)
    for k in range(top):
        spread = spread | (slots[:, None] == target[None, :, k])
    placed = dot(spread.astype(BF16), both, ((1,), (0,))).astype(BF16)
    placed = placed.reshape(experts, pad, 2 * piece)
    arrived = lax.all_to_all(placed, "expert", split_axis=0, concat_axis=0, tiled=True)
    arrived = arrived.reshape(experts, pad, 2, piece).transpose(2, 1, 0, 3).reshape(2, pad, width)

    own_slots = jnp.arange(width, dtype=jnp.int32)
    hit = (target[:, :, None] == me * pad + own_slots[None, None, :]) & (own_slots < cap)[None, None, :]
    own_gates = jnp.sum(jnp.where(hit, gate_values.astype(F32)[:, :, None], 0.0), axis=(0, 1))
    spare = lax.broadcasted_iota(jnp.int32, (pad, width), 0) == cap
    row_block = jnp.where(spare, own_gates.astype(BF16)[None, :], arrived[0])
    grad_block = arrived[1]

    row_all = lax.all_gather(row_block, "dp", axis=0, axis_index_groups=groups)
    grad_all = jnp.zeros((half, pad, width), BF16)
    moving = grad_block
    for step in range(half):
        grad_all = lax.dynamic_update_slice(grad_all, moving[None], ((spot + step) % half, 0, 0))
        if step < half - 1:
            moving = lax.ppermute(moving, "dp", back)
    gates = jnp.pad(row_all[:, cap, :cap].astype(F32), ((0, 0), (0, pad - cap))).reshape(half * pad, 1)
    rows = row_all.reshape(half * pad, width)
    grads = grad_all.reshape(half * pad, width)

    scaled = (gates * grads.astype(F32)).astype(BF16)
    gate_terms = jnp.zeros((half * pad,), F32)
    slopes, lows = [], []
    for first, second in ((own_in, own_out), (mate_in, mate_out)):
        pre = dot(rows, first, ((1,), (0,)))
        raw = dot(grads, second, ((1,), (1,)))
        hidden, slope = gelu_pair(pre)
        gate_terms = gate_terms + jnp.sum(hidden * raw, axis=1)
        slopes.append((gates * raw * slope).astype(BF16))
        lows.append(hidden.astype(BF16))
    row_terms = dot(slopes[0], own_in, ((1,), (1,))) + dot(slopes[1], mate_in, ((1,), (1,)))
    row_terms = row_terms.reshape(half, pad, width)
    gate_terms = jnp.pad(gate_terms.reshape(half, pad)[:, :cap], ((0, 0), (0, ring_cut - cap)))
    spare_row = lax.broadcasted_iota(jnp.int32, (1, pad, 1), 1) == cap
    near = jnp.where(spare_row, gate_terms[:, None, :], row_terms[:, :, :ring_cut])
    far = row_terms[:, :, ring_cut:]

    summed = lax.psum_scatter(near, "dp", scatter_dimension=0, axis_index_groups=groups)
    moving = lax.dynamic_index_in_dim(far, (spot + 1) % half, 0, keepdims=False)
    for step in range(half - 1):
        moving = lax.ppermute(moving, "dp", back)
        moving = moving + lax.dynamic_index_in_dim(far, (spot + 2 + step) % half, 0, keepdims=False)

    mate_first = lax.ppermute(dot(rows, slopes[1], ((0,), (0,))).astype(BF16), "dp", mates)
    mate_second = lax.ppermute(dot(lows[1], scaled, ((0,), (0,))).astype(BF16), "dp", mates)
    grad_first = (dot(rows, slopes[0], ((0,), (0,))) + mate_first.astype(F32)).astype(BF16)
    grad_second = (dot(lows[0], scaled, ((0,), (0,))) + mate_second.astype(F32)).astype(BF16)

    slot_gates = jnp.pad(summed[cap, :cap].astype(BF16), (0, piece - cap))
    grad_rows = jnp.concatenate([summed, moving], axis=1).astype(BF16).reshape(pad, experts, piece)
    grad_rows = grad_rows.transpose(1, 0, 2)
    spare_slot = lax.broadcasted_iota(jnp.int32, (1, pad, 1), 1) == cap
    grad_rows = jnp.where(spare_slot, slot_gates[None, None, :], grad_rows)
    returned = lax.all_to_all(grad_rows, "expert", split_axis=0, concat_axis=0, tiled=True)
    gates_back = jnp.pad(returned[:, cap, :cap], ((0, 0), (0, pad - cap))).reshape(experts * pad)
    returned = returned.reshape(experts * pad, piece)
    gather = jnp.zeros((tok_rows, experts * pad), jnp.bool_)
    gate_out = []
    for k in range(top):
        match = target[:, k, None] == slots[None, :]
        gather = gather | match
        gate_out.append(jnp.sum(jnp.where(match, gates_back.astype(F32)[None, :], 0.0), axis=1))
    token_grads = dot(gather.astype(BF16), returned, ((1,), (0,))).astype(BF16)
    return token_grads, jnp.stack(gate_out, axis=1), grad_first[None], grad_second[None]


def solution(mesh):
    return jax.shard_map(
        body,
        mesh=mesh,
        in_specs=(
            P("dp", "expert"),
            P("dp", "expert"),
            P("dp", None),
            P("dp", None),
            P("dp", None),
            P("dp", None),
            P("expert", None, "dp"),
            P("expert", "dp", None),
        ),
        out_specs=(
            P("dp", "expert"),
            P("dp", None),
            P("expert", None, "dp"),
            P("expert", "dp", None),
        ),
        check_vma=False,
    )
```

```python
import math

import jax
import jax.numpy as jnp
from jax import lax
from jax.sharding import PartitionSpec as P

BF16 = jnp.bfloat16
F32 = jnp.float32


def gelu_pair(values):
    cumul = 0.5 * (1.0 + lax.erf(values * (1.0 / math.sqrt(2.0))))
    density = jnp.exp(-0.5 * values * values) * (1.0 / math.sqrt(2.0 * math.pi))
    return values * cumul, cumul + values * density


def dot(left, right, dims):
    return lax.dot_general(left, right, ((dims[0], dims[1]), ((), ())), preferred_element_type=F32)


def pieces(values, cuts):
    sizes = [values.shape[0] // cuts // 16 * 16] * (cuts - 1)
    sizes.append(values.shape[0] - sum(sizes))
    starts = [sum(sizes[:i]) for i in range(cuts)]
    return [values[at:at + size] for at, size in zip(starts, sizes)]


def body(tokens, cotangent, gate_values, route_ids, route_slots, kept_mask, weight_in, weight_out):
    experts = lax.axis_size("expert")
    dp = lax.axis_size("dp")
    ring = dp // 2
    half = ring // 2
    tok_rows, piece = tokens.shape
    width = piece * experts
    top = route_ids.shape[1]
    cap = (21 * top * tok_rows + 20 * experts - 1) // (20 * experts)
    pad = (cap + 1 + 7) // 8 * 8
    me = lax.axis_index("expert")

    def shift(values, by):
        return lax.ppermute(values, "dp", [(i, (i + by) % dp) for i in range(dp)])

    def swap(values):
        return lax.ppermute(values, "dp", [(i, i ^ 1) for i in range(dp)])

    own_in, own_out = weight_in[0], weight_out[0]
    mate_out = swap(own_out)

    kept = kept_mask == 1
    target = jnp.where(kept, route_ids * pad + route_slots, -1)
    slots = jnp.arange(experts * pad, dtype=jnp.int32)
    both = jnp.concatenate([tokens, cotangent], axis=1)
    spread = jnp.zeros((experts * pad, tok_rows), jnp.bool_)
    for k in range(top):
        spread = spread | (slots[:, None] == target[None, :, k])
    placed = dot(spread.astype(BF16), both, ((1,), (0,))).astype(BF16)
    placed = placed.reshape(experts, pad, 2 * piece)
    arrived = lax.all_to_all(placed, "expert", split_axis=0, concat_axis=0, tiled=True)
    arrived = arrived.reshape(experts, pad, 2, piece).transpose(1, 2, 0, 3).reshape(pad, 2 * width)

    own_slots = jnp.arange(2 * width, dtype=jnp.int32)
    hit = (target[:, :, None] == me * pad + own_slots[None, None, :]) & (own_slots < cap)[None, None, :]
    own_gates = jnp.sum(jnp.where(hit, gate_values.astype(F32)[:, :, None], 0.0), axis=(0, 1))
    spare = lax.broadcasted_iota(jnp.int32, (pad, 2 * width), 0) == cap
    block = jnp.where(spare, own_gates.astype(BF16)[None, :], arrived)

    found = {0: block}
    ahead = behind = block
    queue, mate_in = pieces(own_in, 4), []
    for step in range(half):
        sent = [queue.pop(0)] if queue and step > 0 else []
        ahead, behind, *sent = lax.optimization_barrier((ahead, behind, *sent))
        ahead = shift(ahead, 2)
        found[-step - 1] = ahead
        if step + 1 < ring - half:
            behind = shift(behind, -2)
            found[step + 1] = behind
        if sent:
            got = swap(sent[0])
            ahead, behind, got = lax.optimization_barrier((ahead, behind, got))
            mate_in.append(got)
    while queue:
        mate_in.append(swap(queue.pop(0)))
    mate_in = jnp.concatenate(mate_in, axis=0)
    order = sorted(found)
    gathered = jnp.stack([found[at] for at in order])
    gates = jnp.pad(gathered[:, cap, :cap].astype(F32), ((0, 0), (0, pad - cap))).reshape(ring * pad, 1)
    gathered = gathered.reshape(ring * pad, 2 * width)
    rows, grads = gathered[:, :width], gathered[:, width:]

    gate_terms = jnp.zeros((ring * pad,), F32)
    slopes, lows = [], []
    for first, second in ((own_in, own_out), (mate_in, mate_out)):
        pre = dot(rows, first, ((1,), (0,)))
        raw = dot(grads, second, ((1,), (1,)))
        hidden, slope = gelu_pair(pre)
        gate_terms = gate_terms + jnp.sum(hidden * raw, axis=1)
        slopes.append((gates * raw * slope).astype(BF16))
        lows.append(hidden.astype(BF16))
    row_terms = dot(slopes[0], own_in, ((1,), (1,))) + dot(slopes[1], mate_in, ((1,), (1,)))
    row_terms = row_terms.reshape(ring, pad, width)
    gate_terms = jnp.pad(gate_terms.reshape(ring, pad)[:, :cap], ((0, 0), (0, width - cap)))
    spare_row = lax.broadcasted_iota(jnp.int32, (1, pad, 1), 1) == cap
    terms = jnp.where(spare_row, gate_terms[:, None, :], row_terms)
    part = {at: terms[i] for i, at in enumerate(order)}

    scaled = (gates * grads.astype(F32)).astype(BF16)
    queue = pieces(dot(rows, slopes[1], ((0,), (0,))).astype(BF16), 4)
    queue += pieces(dot(lows[1], scaled, ((0,), (0,))).astype(BF16), 3)
    swapped = []
    plus, minus = part[-half], part[ring - half - 1]
    for step in range(half):
        sent = [queue.pop(0)] if queue and step > 0 else []
        plus, minus, *sent = lax.optimization_barrier((plus, minus, *sent))
        at = half - 1 - step
        plus = shift(plus, -2)
        if step > 0:
            minus = shift(minus, 2)
        if sent:
            got = swap(sent[0])
            plus, minus, got = lax.optimization_barrier((plus, minus, got))
            swapped.append(got)
        if at > 0:
            plus = plus + part[-at]
        if step > 0 and at > 0:
            minus = minus + part[at]
    summed = plus + minus + part[0]
    while queue:
        swapped.append(swap(queue.pop(0)))
    mate_first = jnp.concatenate(swapped[:4], axis=0)
    mate_second = jnp.concatenate(swapped[4:], axis=0)
    grad_first = (dot(rows, slopes[0], ((0,), (0,))) + mate_first.astype(F32)).astype(BF16)
    grad_second = (dot(lows[0], scaled, ((0,), (0,))) + mate_second.astype(F32)).astype(BF16)

    slot_gates = jnp.pad(summed[cap, :cap].astype(BF16), (0, piece - cap))
    grad_rows = summed.astype(BF16).reshape(pad, experts, piece).transpose(1, 0, 2)
    spare_slot = lax.broadcasted_iota(jnp.int32, (1, pad, 1), 1) == cap
    grad_rows = jnp.where(spare_slot, slot_gates[None, None, :], grad_rows)
    returned = lax.all_to_all(grad_rows, "expert", split_axis=0, concat_axis=0, tiled=True)
    gates_back = jnp.pad(returned[:, cap, :cap], ((0, 0), (0, pad - cap))).reshape(experts * pad)
    returned = returned.reshape(experts * pad, piece)
    gather = jnp.zeros((tok_rows, experts * pad), jnp.bool_)
    gate_out = []
    for k in range(top):
        match = target[:, k, None] == slots[None, :]
        gather = gather | match
        gate_out.append(jnp.sum(jnp.where(match, gates_back.astype(F32)[None, :], 0.0), axis=1))
    token_grads = dot(gather.astype(BF16), returned, ((1,), (0,))).astype(BF16)
    return token_grads, jnp.stack(gate_out, axis=1), grad_first[None], grad_second[None]


def solution(mesh):
    return jax.shard_map(
        body,
        mesh=mesh,
        in_specs=(
            P("dp", "expert"),
            P("dp", "expert"),
            P("dp", None),
            P("dp", None),
            P("dp", None),
            P("dp", None),
            P("expert", None, "dp"),
            P("expert", "dp", None),
        ),
        out_specs=(
            P("dp", "expert"),
            P("dp", None),
            P("expert", None, "dp"),
            P("expert", "dp", None),
        ),
        check_vma=False,
    )
```

```python
import math

import jax
import jax.numpy as jnp
from jax import lax
from jax.sharding import PartitionSpec as P

BF16 = jnp.bfloat16
F32 = jnp.float32


def gelu_pair(values):
    cumul = 0.5 * (1.0 + lax.erf(values * (1.0 / math.sqrt(2.0))))
    density = jnp.exp(-0.5 * values * values) * (1.0 / math.sqrt(2.0 * math.pi))
    return values * cumul, cumul + values * density


def dot(left, right, dims):
    return lax.dot_general(left, right, ((dims[0], dims[1]), ((), ())), preferred_element_type=F32)


def body(tokens, cotangent, gate_values, route_ids, route_slots, kept_mask, weight_in, weight_out):
    experts = lax.axis_size("expert")
    dp = lax.axis_size("dp")
    ring = dp // 2
    groups = [list(range(0, dp, 2)), list(range(1, dp, 2))]
    tok_rows, piece = tokens.shape
    width = piece * experts
    top = route_ids.shape[1]
    cap = (21 * top * tok_rows + 20 * experts - 1) // (20 * experts)
    pad = (cap + 1 + 7) // 8 * 8
    me = lax.axis_index("expert")

    def swap(values):
        return lax.ppermute(values, "dp", [(i, i ^ 1) for i in range(dp)])

    own_in, own_out = weight_in[0], weight_out[0]
    mate_in, mate_out = swap(own_in), swap(own_out)

    kept = kept_mask == 1
    target = jnp.where(kept, route_ids * pad + route_slots, -1)
    slots = jnp.arange(experts * pad, dtype=jnp.int32)
    both = jnp.concatenate([tokens, cotangent], axis=1)
    spread = jnp.zeros((experts * pad, tok_rows), jnp.bool_)
    for k in range(top):
        spread = spread | (slots[:, None] == target[None, :, k])
    placed = dot(spread.astype(BF16), both, ((1,), (0,))).astype(BF16)
    placed = placed.reshape(experts, pad, 2 * piece)
    arrived = lax.all_to_all(placed, "expert", split_axis=0, concat_axis=0, tiled=True)
    arrived = arrived.reshape(experts, pad, 2, piece).transpose(1, 2, 0, 3).reshape(pad, 2 * width)

    own_slots = jnp.arange(2 * width, dtype=jnp.int32)
    hit = (target[:, :, None] == me * pad + own_slots[None, None, :]) & (own_slots < cap)[None, None, :]
    own_gates = jnp.sum(jnp.where(hit, gate_values.astype(F32)[:, :, None], 0.0), axis=(0, 1))
    spare = lax.broadcasted_iota(jnp.int32, (pad, 2 * width), 0) == cap
    block = jnp.where(spare, own_gates.astype(BF16)[None, :], arrived)

    gathered = lax.all_gather(block, "dp", axis=0, axis_index_groups=groups)
    gates = jnp.pad(gathered[:, cap, :cap].astype(F32), ((0, 0), (0, pad - cap))).reshape(ring * pad, 1)
    gathered = gathered.reshape(ring * pad, 2 * width)
    rows, grads = gathered[:, :width], gathered[:, width:]

    gate_terms = jnp.zeros((ring * pad,), F32)
    slopes, lows = [], []
    for first, second in ((own_in, own_out), (mate_in, mate_out)):
        pre = dot(rows, first, ((1,), (0,)))
        raw = dot(grads, second, ((1,), (1,)))
        hidden, slope = gelu_pair(pre)
        gate_terms = gate_terms + jnp.sum(hidden * raw, axis=1)
        slopes.append((gates * raw * slope).astype(BF16))
        lows.append(hidden.astype(BF16))
    row_terms = dot(slopes[0], own_in, ((1,), (1,))) + dot(slopes[1], mate_in, ((1,), (1,)))
    row_terms = row_terms.reshape(ring, pad, width)
    gate_terms = jnp.pad(gate_terms.reshape(ring, pad)[:, :cap], ((0, 0), (0, width - cap)))
    spare_row = lax.broadcasted_iota(jnp.int32, (1, pad, 1), 1) == cap
    terms = jnp.where(spare_row, gate_terms[:, None, :], row_terms)
    summed = lax.psum_scatter(terms, "dp", scatter_dimension=0, axis_index_groups=groups)

    scaled = (gates * grads.astype(F32)).astype(BF16)
    mate_first = swap(dot(rows, slopes[1], ((0,), (0,))).astype(BF16))
    mate_second = swap(dot(lows[1], scaled, ((0,), (0,))).astype(BF16))
    grad_first = (dot(rows, slopes[0], ((0,), (0,))) + mate_first.astype(F32)).astype(BF16)
    grad_second = (dot(lows[0], scaled, ((0,), (0,))) + mate_second.astype(F32)).astype(BF16)

    slot_gates = jnp.pad(summed[cap, :cap].astype(BF16), (0, piece - cap))
    grad_rows = summed.astype(BF16).reshape(pad, experts, piece).transpose(1, 0, 2)
    spare_slot = lax.broadcasted_iota(jnp.int32, (1, pad, 1), 1) == cap
    grad_rows = jnp.where(spare_slot, slot_gates[None, None, :], grad_rows)
    returned = lax.all_to_all(grad_rows, "expert", split_axis=0, concat_axis=0, tiled=True)
    gates_back = jnp.pad(returned[:, cap, :cap], ((0, 0), (0, pad - cap))).reshape(experts * pad)
    returned = returned.reshape(experts * pad, piece)
    gather = jnp.zeros((tok_rows, experts * pad), jnp.bool_)
    gate_out = []
    for k in range(top):
        match = target[:, k, None] == slots[None, :]
        gather = gather | match
        gate_out.append(jnp.sum(jnp.where(match, gates_back.astype(F32)[None, :], 0.0), axis=1))
    token_grads = dot(gather.astype(BF16), returned, ((1,), (0,))).astype(BF16)
    return token_grads, jnp.stack(gate_out, axis=1), grad_first[None], grad_second[None]


def solution(mesh):
    return jax.shard_map(
        body,
        mesh=mesh,
        in_specs=(
            P("dp", "expert"),
            P("dp", "expert"),
            P("dp", None),
            P("dp", None),
            P("dp", None),
            P("dp", None),
            P("expert", None, "dp"),
            P("expert", "dp", None),
        ),
        out_specs=(
            P("dp", "expert"),
            P("dp", None),
            P("expert", None, "dp"),
            P("expert", "dp", None),
        ),
        check_vma=False,
    )
```

```python
import math

import jax
import jax.numpy as jnp
from jax import lax
from jax.sharding import PartitionSpec as P

BF16 = jnp.bfloat16
F32 = jnp.float32


def gelu_pair(values):
    cumul = 0.5 * (1.0 + lax.erf(values * (1.0 / math.sqrt(2.0))))
    density = jnp.exp(-0.5 * values * values) * (1.0 / math.sqrt(2.0 * math.pi))
    return values * cumul, cumul + values * density


def dot(left, right, dims):
    return lax.dot_general(left, right, ((dims[0], dims[1]), ((), ())), preferred_element_type=F32)


def body(tokens, cotangent, gate_values, route_ids, route_slots, kept_mask, weight_in, weight_out):
    experts = lax.axis_size("expert")
    dp = lax.axis_size("dp")
    ring = dp // 2
    groups = [list(range(0, dp, 2)), list(range(1, dp, 2))]
    tok_rows, piece = tokens.shape
    width = piece * experts
    top = route_ids.shape[1]
    cap = (21 * top * tok_rows + 20 * experts - 1) // (20 * experts)
    pad = (cap + 1 + 7) // 8 * 8
    me = lax.axis_index("expert")

    def swap(values):
        return lax.ppermute(values, "dp", [(i, i ^ 1) for i in range(dp)])

    own_in, own_out = weight_in[0], weight_out[0]
    mate_in, mate_out = swap(own_in), swap(own_out)

    kept = kept_mask == 1
    target = jnp.where(kept, route_ids * pad + route_slots, -1)
    slots = jnp.arange(experts * pad, dtype=jnp.int32)
    lanes = (2 * piece + 127) // 128 * 128
    both = jnp.pad(jnp.concatenate([tokens, cotangent], axis=1), ((0, 0), (0, lanes - 2 * piece)))
    spread = jnp.zeros((experts * pad, tok_rows), jnp.bool_)
    for k in range(top):
        spread = spread | (slots[:, None] == target[None, :, k])
    placed = dot(spread.astype(BF16), both, ((1,), (0,))).astype(BF16)
    placed = placed.reshape(experts, pad, lanes)
    arrived = lax.all_to_all(placed, "expert", split_axis=0, concat_axis=0, tiled=True)
    arrived = arrived[:, :, : 2 * piece].reshape(experts, pad, 2, piece).transpose(1, 2, 0, 3).reshape(pad, 2 * width)

    own_slots = jnp.arange(2 * width, dtype=jnp.int32)
    hit = (target[:, :, None] == me * pad + own_slots[None, None, :]) & (own_slots < cap)[None, None, :]
    own_gates = jnp.sum(jnp.where(hit, gate_values.astype(F32)[:, :, None], 0.0), axis=(0, 1))
    spare = lax.broadcasted_iota(jnp.int32, (pad, 2 * width), 0) == cap
    block = jnp.where(spare, own_gates.astype(BF16)[None, :], arrived)

    gathered = lax.all_gather(block, "dp", axis=0, axis_index_groups=groups)
    gates = jnp.pad(gathered[:, cap, :cap].astype(F32), ((0, 0), (0, pad - cap))).reshape(ring * pad, 1)
    gathered = gathered.reshape(ring * pad, 2 * width)
    rows, grads = gathered[:, :width], gathered[:, width:]

    gate_terms = jnp.zeros((ring * pad,), F32)
    slopes, lows = [], []
    for first, second in ((own_in, own_out), (mate_in, mate_out)):
        pre = dot(rows, first, ((1,), (0,)))
        raw = dot(grads, second, ((1,), (1,)))
        hidden, slope = gelu_pair(pre)
        gate_terms = gate_terms + jnp.sum(hidden * raw, axis=1)
        slopes.append((gates * raw * slope).astype(BF16))
        lows.append(hidden.astype(BF16))
    row_terms = dot(slopes[0], own_in, ((1,), (1,))) + dot(slopes[1], mate_in, ((1,), (1,)))
    row_terms = row_terms.reshape(ring, pad, width)
    gate_terms = jnp.pad(gate_terms.reshape(ring, pad)[:, :cap], ((0, 0), (0, width - cap)))
    spare_row = lax.broadcasted_iota(jnp.int32, (1, pad, 1), 1) == cap
    terms = jnp.where(spare_row, gate_terms[:, None, :], row_terms)
    summed = lax.psum_scatter(terms, "dp", scatter_dimension=0, axis_index_groups=groups)

    scaled = (gates * grads.astype(F32)).astype(BF16)
    mate_first = swap(dot(rows, slopes[1], ((0,), (0,))).astype(BF16))
    mate_second = swap(dot(lows[1], scaled, ((0,), (0,))).astype(BF16))
    grad_first = (dot(rows, slopes[0], ((0,), (0,))) + mate_first.astype(F32)).astype(BF16)
    grad_second = (dot(lows[0], scaled, ((0,), (0,))) + mate_second.astype(F32)).astype(BF16)

    grad_rows = summed.astype(BF16).reshape(pad, experts, piece).transpose(1, 0, 2)
    slot_gates = jnp.pad(grad_rows[0, cap, :cap], (0, pad - cap))
    out_lanes = (piece + 1 + 127) // 128 * 128
    grad_rows = jnp.pad(grad_rows, ((0, 0), (0, 0), (0, out_lanes - piece)))
    lane = lax.broadcasted_iota(jnp.int32, (1, 1, out_lanes), 2)
    grad_rows = jnp.where(lane == piece, slot_gates[None, :, None], grad_rows)
    returned = lax.all_to_all(grad_rows, "expert", split_axis=0, concat_axis=0, tiled=True)
    returned = returned.reshape(experts * pad, out_lanes)
    spots = jnp.concatenate([target[:, k] for k in range(top)], axis=0)
    match = (spots[:, None] == slots[None, :]).astype(BF16)
    taken = dot(match, returned, ((1,), (0,))).reshape(top, tok_rows, out_lanes)
    token_grads = jnp.sum(taken[:, :, :piece], axis=0).astype(BF16)
    return token_grads, taken[:, :, piece].T, grad_first[None], grad_second[None]


def solution(mesh):
    return jax.shard_map(
        body,
        mesh=mesh,
        in_specs=(
            P("dp", "expert"),
            P("dp", "expert"),
            P("dp", None),
            P("dp", None),
            P("dp", None),
            P("dp", None),
            P("expert", None, "dp"),
            P("expert", "dp", None),
        ),
        out_specs=(
            P("dp", "expert"),
            P("dp", None),
            P("expert", None, "dp"),
            P("expert", "dp", None),
        ),
        check_vma=False,
    )
```

```python
import math

import jax
import jax.numpy as jnp
from jax import lax
from jax.sharding import PartitionSpec as P

BF16 = jnp.bfloat16
F32 = jnp.float32


def gelu_pair(values):
    cumul = 0.5 * (1.0 + lax.erf(values * (1.0 / math.sqrt(2.0))))
    density = jnp.exp(-0.5 * values * values) * (1.0 / math.sqrt(2.0 * math.pi))
    return values * cumul, cumul + values * density


def dot(left, right, dims):
    return lax.dot_general(left, right, ((dims[0], dims[1]), ((), ())), preferred_element_type=F32)


def body(tokens, cotangent, gate_values, route_ids, route_slots, kept_mask, weight_in, weight_out):
    experts = lax.axis_size("expert")
    dp = lax.axis_size("dp")
    ring = dp // 2
    groups = [list(range(0, dp, 2)), list(range(1, dp, 2))]
    tok_rows, piece = tokens.shape
    width = piece * experts
    top = route_ids.shape[1]
    cap = (21 * top * tok_rows + 20 * experts - 1) // (20 * experts)
    pad = (cap + 1 + 7) // 8 * 8
    me = lax.axis_index("expert")

    def swap(values):
        return lax.ppermute(values, "dp", [(i, i ^ 1) for i in range(dp)])

    own_in, own_out = weight_in[0], weight_out[0]
    mate_in, mate_out = swap(own_in), swap(own_out)

    kept = kept_mask == 1
    target = jnp.where(kept, route_ids * pad + route_slots, -1)
    slots = jnp.arange(experts * pad, dtype=jnp.int32)
    lanes = (2 * piece + 127) // 128 * 128
    both = jnp.pad(jnp.concatenate([tokens, cotangent], axis=1), ((0, 0), (0, lanes - 2 * piece)))
    spread = jnp.zeros((experts * pad, tok_rows), jnp.bool_)
    for k in range(top):
        spread = spread | (slots[:, None] == target[None, :, k])
    placed = dot(spread.astype(BF16), both, ((1,), (0,))).astype(BF16)
    placed = placed.reshape(experts, pad, lanes)
    arrived = lax.all_to_all(placed, "expert", split_axis=0, concat_axis=0, tiled=True)
    arrived = arrived[:, :, : 2 * piece].reshape(experts, pad, 2, piece).transpose(1, 2, 0, 3).reshape(pad, 2 * width)

    own_slots = jnp.arange(2 * width, dtype=jnp.int32)
    hit = (target[:, :, None] == me * pad + own_slots[None, None, :]) & (own_slots < cap)[None, None, :]
    own_gates = jnp.sum(jnp.where(hit, gate_values.astype(F32)[:, :, None], 0.0), axis=(0, 1))
    spare = lax.broadcasted_iota(jnp.int32, (pad, 2 * width), 0) == cap
    block = jnp.where(spare, own_gates.astype(BF16)[None, :], arrived)

    gathered = lax.all_gather(block, "dp", axis=0, axis_index_groups=groups)
    gates = jnp.pad(gathered[:, cap, :cap].astype(F32), ((0, 0), (0, pad - cap))).reshape(ring * pad, 1)
    gathered = gathered.reshape(ring * pad, 2 * width)
    rows, grads = gathered[:, :width], gathered[:, width:]

    gate_terms = jnp.zeros((ring * pad,), F32)
    slopes, lows = [], []
    for first, second in ((own_in, own_out), (mate_in, mate_out)):
        pre = dot(rows, first, ((1,), (0,)))
        raw = dot(grads, second, ((1,), (1,)))
        hidden, slope = gelu_pair(pre)
        gate_terms = gate_terms + jnp.sum(hidden * raw, axis=1)
        slopes.append((gates * raw * slope).astype(BF16))
        lows.append(hidden.astype(BF16))
    row_terms = dot(slopes[0], own_in, ((1,), (1,))) + dot(slopes[1], mate_in, ((1,), (1,)))
    row_terms = row_terms.reshape(ring, pad, width)
    gate_terms = jnp.pad(gate_terms.reshape(ring, pad)[:, :cap], ((0, 0), (0, width - cap)))
    spare_row = lax.broadcasted_iota(jnp.int32, (1, pad, 1), 1) == cap
    terms = jnp.where(spare_row, gate_terms[:, None, :], row_terms)
    summed = lax.psum_scatter(terms, "dp", scatter_dimension=0, axis_index_groups=groups)

    scaled = (gates * grads.astype(F32)).astype(BF16)
    mate_first = swap(dot(rows, slopes[1], ((0,), (0,))).astype(BF16))
    mate_second = swap(dot(lows[1], scaled, ((0,), (0,))).astype(BF16))
    grad_first = (dot(rows, slopes[0], ((0,), (0,))) + mate_first.astype(F32)).astype(BF16)
    grad_second = (dot(lows[0], scaled, ((0,), (0,))) + mate_second.astype(F32)).astype(BF16)

    grad_rows = summed.astype(BF16).reshape(pad, experts, piece).transpose(1, 0, 2)
    slot_gates = jnp.pad(grad_rows[0, cap, :cap], (0, pad - cap))
    out_lanes = (piece + 1 + 127) // 128 * 128
    grad_rows = jnp.pad(grad_rows, ((0, 0), (0, 0), (0, out_lanes - piece)))
    lane = lax.broadcasted_iota(jnp.int32, (1, 1, out_lanes), 2)
    grad_rows = jnp.where(lane == piece, slot_gates[None, :, None], grad_rows)
    returned = lax.all_to_all(grad_rows, "expert", split_axis=0, concat_axis=0, tiled=True)
    returned = returned.reshape(experts * pad, out_lanes)
    spots = jnp.concatenate([target[:, k] for k in range(top)], axis=0)
    match = (spots[:, None] == slots[None, :]).astype(BF16)
    taken = dot(returned, match, ((0,), (1,))).reshape(out_lanes, top, tok_rows)
    token_grads = jnp.sum(taken[:piece], axis=1).astype(BF16).T
    return token_grads, taken[piece].T, grad_first[None], grad_second[None]


def solution(mesh):
    return jax.shard_map(
        body,
        mesh=mesh,
        in_specs=(
            P("dp", "expert"),
            P("dp", "expert"),
            P("dp", None),
            P("dp", None),
            P("dp", None),
            P("dp", None),
            P("expert", None, "dp"),
            P("expert", "dp", None),
        ),
        out_specs=(
            P("dp", "expert"),
            P("dp", None),
            P("expert", None, "dp"),
            P("expert", "dp", None),
        ),
        check_vma=False,
    )
```
